32 devices in a mesh: dp: 16 (over z, y, x), mp: 2 (over core).
Axes of the slice: x: 2, y: 2, z: 4, core: 2. Of those that a mesh axis runs over, the one named last changes fastest.
Arguments:
- tokens: bfloat16 [10240, 1152], P('dp'), may hold values from -6 to 6
- time_token: bfloat16 [32, 1152], P('dp'), may hold values from -6 to 6
- lengths: int32 [32], P('dp'), may hold values from 192 to 320, as said below
- rel_index: int32 [320, 320], replicated, may hold values from 0 to 960
- w_query: bfloat16 [1152, 1152], P('dp', 'mp'), may hold values from -0.1875 to 0.1875
- w_key: bfloat16 [1152, 1152], P('dp', 'mp'), may hold values from -0.1875 to 0.1875
- w_value: bfloat16 [1152, 1152], P('dp', 'mp'), may hold values from -0.1875 to 0.1875
- t_query: bfloat16 [1152, 1152], P('dp', 'mp'), may hold values from -0.1875 to 0.1875
- t_value: bfloat16 [1152, 1152], P('dp', 'mp'), may hold values from -0.1875 to 0.1875
- w_out: bfloat16 [1152, 1152], P('mp', 'dp'), may hold values from -0.75 to 0.75
- w_up: bfloat16 [1152, 4608], P('dp', 'mp'), may hold values from -0.1875 to 0.1875
- w_down: bfloat16 [4608, 1152], P('mp', 'dp'), may hold values from -0.125 to 0.125
- b_up: float32 [4608], P('mp'), may hold values from -1.8 to 1.8
- b_down: float32 [1152], replicated, may hold values from -1.8 to 1.8
- ln1_gain: float32 [1152], replicated, may hold values from 0.5 to 1.5
- ln1_bias: float32 [1152], replicated, may hold values from -1.8 to 1.8
- ln2_gain: float32 [1152], replicated, may hold values from 0.5 to 1.5
- ln2_bias: float32 [1152], replicated, may hold values from -1.8 to 1.8
- bias_table: float32 [16, 961], P('mp'), may hold values from -5 to 5
- cotangent: bfloat16 [10240, 1152], P('dp'), may hold values from -6 to 6
Outputs:
- block_out: bfloat16 [10240, 1152], P('dp')
- grad_input: float32 [10240, 1152], P('dp')
- grad_time: float32 [32, 1152], P('dp')
- grad_w_query: float32 [1152, 1152], P('dp', 'mp')
- grad_w_key: float32 [1152, 1152], P('dp', 'mp')
- grad_w_value: float32 [1152, 1152], P('dp', 'mp')
- grad_t_query: float32 [1152, 1152], P('dp', 'mp')
- grad_t_value: float32 [1152, 1152], P('dp', 'mp')
- grad_w_out: float32 [1152, 1152], P('mp', 'dp')
- grad_w_up: float32 [1152, 4608], P('dp', 'mp')
- grad_w_down: float32 [4608, 1152], P('mp', 'dp')
- grad_b_up: float32 [4608], P('mp')
- grad_b_down: float32 [1152], replicated
- grad_ln1_gain: float32 [1152], replicated
- grad_ln1_bias: float32 [1152], replicated
- grad_ln2_gain: float32 [1152], replicated
- grad_ln2_bias: float32 [1152], replicated
- grad_bias_table: float32 [16, 961], P('mp')
The draws below stay inside these ranges and needn't reach their ends.
Inputs may be any that keep to these rules, and one draw needn't show every extreme that they name: `lengths`: some image has exactly 320 real tokens and some exactly 192.
All inputs are finite; a program needn't handle non-finite values.
Results may differ from the reference program's by a relative error of at most 0.015.
Values may be sent and summed in bfloat16 or wider, within the bound.
A program may use at most 320 MiB of HBM per device.

```python
import math
import jax
import jax.numpy as jnp
from jax import lax

D = 1152
HEADS = 16
HD = 72
FF = 4608
LMAX = 320
LMIN = 192
NREL = 961
IMAGES = 32
TOKENS = 10240


def draw_lengths(key, part):
    key = jax.random.fold_in(key, 7)
    first_key, second_key = jax.random.split(key)
    lengths_drawn = jax.random.randint(first_key, (IMAGES,), LMIN, LMAX + 1)
    shuffled = jax.random.permutation(second_key, IMAGES)
    positions = jnp.arange(IMAGES)
    lengths_drawn = jnp.where(positions == shuffled[0], LMAX, lengths_drawn)
    lengths_drawn = jnp.where(positions == shuffled[1], LMIN, lengths_drawn)
    return lengths_drawn.astype(jnp.int32)


def set_ends(drawn, rng, low, top_value):
    longest = drawn.shape.index(max(drawn.shape))
    spots = []
    for shift in (0, 1):
        where = [jax.random.randint(jax.random.fold_in(rng, axis), (), 0, length) for axis, length in enumerate(drawn.shape)]
        where[longest] = (where[longest] + shift) % drawn.shape[longest]
        spots.append(tuple(where))
    return drawn.at[spots[0]].set(low).at[spots[1]].set(top_value)


def spiked(values, rng, source, target, parts, factor):
    def block_of(dim):
        return (jnp.arange(values.shape[dim]) // (values.shape[dim] // parts)).reshape((-1,) + (1,) * (values.ndim - 1 - dim))

    near = jax.random.permutation(rng, parts)[block_of(target)]
    second = (block_of(target) + parts // 2) % parts
    return jnp.where((block_of(source) == near) | (block_of(source) == second), factor * values, values)


def level_of(stream_key, dims, cuts, low, largest):
    def one(axis_at, parts):
        steps = jax.random.uniform(jax.random.fold_in(jax.random.fold_in(stream_key, 6), axis_at), (parts,), jnp.float32, low / len(cuts), largest / len(cuts))
        return jnp.repeat(jnp.exp(steps), dims[axis_at] // parts).reshape((-1,) + (1,) * (len(dims) - axis_at - 1))

    loudness = one(*cuts[0])
    for cut in cuts[1:]:
        loudness = loudness * one(*cut)
    return loudness


def bell_draw(rng, dims, scale, limit, cuts=(), held_as=jnp.bfloat16):
    loudness = level_of(rng, dims, cuts, -0.22, 0.18) if cuts else 1.0
    values = jax.random.normal(rng, dims, jnp.float32) * scale * loudness
    return jnp.minimum(jnp.maximum(values, -limit), limit).astype(held_as)


def heavy_noise(rng, shape, deviation, bound, cuts, heavy, held_as=jnp.bfloat16):
    entries = deviation * jax.random.normal(rng, shape, jnp.float32)
    if cuts:
        entries = entries * level_of(rng, shape, cuts, -0.22, 0.18)
    return jnp.clip(spiked(entries, jax.random.fold_in(rng, 3), *heavy), -bound, bound).astype(held_as)


def setup_inputs(seed: int = 0) -> dict:
    arg_keys = jax.random.split(jax.random.key(seed), 21)
    return {
        "tokens": bell_draw(arg_keys[0], (TOKENS, D), 1.0, 6.0, ((0, 16),)),
        "time_token": bell_draw(arg_keys[1], (IMAGES, D), 1.0, 6.0, ((0, 16),)),
        "lengths": draw_lengths(jax.random.fold_in(arg_keys[20], 71), 0),
        "rel_index": set_ends(jax.random.randint(arg_keys[3], (LMAX, LMAX), 0, NREL), jax.random.fold_in(arg_keys[3], 1), 0, NREL - 1).astype(jnp.int32),
        "w_query": bell_draw(arg_keys[4], (D, D), D ** -0.5, 0.1875, ((0, 16), (1, 2))),
        "w_key": bell_draw(arg_keys[5], (D, D), D ** -0.5, 0.1875, ((0, 16), (1, 2))),
        "w_value": bell_draw(arg_keys[6], (D, D), D ** -0.5, 0.1875, ((0, 16), (1, 2))),
        "t_query": bell_draw(arg_keys[7], (D, D), D ** -0.5, 0.1875, ((0, 16), (1, 2))),
        "t_value": bell_draw(arg_keys[8], (D, D), D ** -0.5, 0.1875, ((0, 16), (1, 2))),
        "w_out": bell_draw(arg_keys[9], (D, D), (D // 16) ** -0.5, 0.75, ((0, 2), (1, 16))),
        "w_up": bell_draw(arg_keys[10], (D, FF), D ** -0.5, 0.1875, ((0, 16), (1, 2))),
        "w_down": bell_draw(arg_keys[11], (FF, D), (FF // 2) ** -0.5, 0.125, ((0, 2), (1, 16))),
        "b_up": bell_draw(arg_keys[12], (FF,), 0.3, 1.8, ((0, 2),), jnp.float32),
        "b_down": bell_draw(arg_keys[13], (D,), 0.3, 1.8, (), jnp.float32),
        "ln1_gain": jnp.clip(1.0 + 0.1 * jax.random.normal(arg_keys[14], (D,), jnp.float32), 0.5, 1.5),
        "ln1_bias": bell_draw(arg_keys[15], (D,), 0.3, 1.8, (), jnp.float32),
        "ln2_gain": jnp.clip(1.0 + 0.1 * jax.random.normal(arg_keys[16], (D,), jnp.float32), 0.5, 1.5),
        "ln2_bias": bell_draw(arg_keys[17], (D,), 0.3, 1.8, (), jnp.float32),
        "bias_table": bell_draw(arg_keys[18], (HEADS, NREL), 1.0, 5.0, ((0, 2),), jnp.float32),
        "cotangent": heavy_noise(arg_keys[19], (TOKENS, D), 1.0, 6.0, ((0, 16),), (0, 1, 16, 2.0)),
    }


HIGH = lax.Precision.HIGHEST
NEG = -1e+30
EPS = 1e-06

@jax.custom_vjp
def low(v):
    return lax.optimization_barrier(v.astype(jnp.bfloat16)).astype(jnp.float32)

@jax.custom_vjp
def low_back(v):
    return v

def low_keep(v):
    return (low(v), None)

def low_pass(kept, grad):
    return (grad,)

def back_keep(v):
    return (v, None)

def back_low(kept, grad):
    return (low(grad),)
low.defvjp(low_keep, low_pass)
low_back.defvjp(back_keep, back_low)

def norm_rows(token_rows, norm_gain, norm_bias):
    centre = lax.optimization_barrier(jnp.mean(token_rows, axis=-1, keepdims=True))
    centred = token_rows - centre
    spread = lax.optimization_barrier(jnp.mean(centred * centred, axis=-1, keepdims=True))
    return centred * lax.rsqrt(spread + EPS) * norm_gain + norm_bias

def reference(tokens, time_token, lengths, rel_index, w_query, w_key, w_value, t_query, t_value, w_out, w_up, w_down, b_up, b_down, ln1_gain, ln1_bias, ln2_gain, ln2_bias, bias_table, cotangent):
    group = math.gcd(IMAGES, 8)
    blocks = IMAGES // group
    score_scale = HD ** (-0.5)
    primals = tuple((entry.astype(jnp.float32) for entry in (tokens, time_token, w_query, w_key, w_value, t_query, t_value, w_out, w_up, w_down, b_up, b_down, ln1_gain, ln1_bias, ln2_gain, ln2_bias, bias_table)))
    group_lengths = lengths.reshape(blocks, group)

    def forward(token_rows, time_rows, query_weight, key_weight, value_weight, query_time, value_time, out_weight, up_weight, down_weight, up_bias, down_bias, gain_one, bias_one, gain_two, bias_two, table):
        bias_rows = table[:, rel_index]

        def one_group(pieces):
            image_rows, image_times, image_lengths = pieces
            is_valid = jnp.arange(LMAX)[None, :] < image_lengths[:, None]
            normed_one = low(norm_rows(image_rows, gain_one, bias_one))

            def project(weight, time_weight):
                direct = jnp.einsum('gld,de->gle', normed_one, weight, precision=HIGH)
                from_time = jnp.dot(image_times, time_weight, precision=HIGH)
                return low(low_back(direct + from_time[:, None, :])).reshape(group, LMAX, HEADS, HD)
            query_rows = project(query_weight, query_time)
            key_direct = jnp.einsum('gld,de->gle', normed_one, key_weight, precision=HIGH)
            key_rows = low(low_back(key_direct)).reshape(group, LMAX, HEADS, HD)
            value_rows = project(value_weight, value_time)
            scores = jnp.einsum('gqhe,gkhe->ghqk', query_rows, key_rows, precision=HIGH) * score_scale + bias_rows[None]
            scores = low_back(scores)
            scores = jnp.where(is_valid[:, None, None, :], scores, NEG)
            highest = lax.optimization_barrier(jnp.max(scores, axis=-1, keepdims=True))
            powers = jnp.exp(scores - highest)
            attn_probs = low(powers / lax.optimization_barrier(jnp.sum(powers, axis=-1, keepdims=True)))
            heads_out = jnp.einsum('ghqk,gkhe->gqhe', attn_probs, value_rows, precision=HIGH).reshape(group, LMAX, D)
            heads_out = low(low_back(heads_out))
            middle = image_rows + low_back(jnp.einsum('gle,ed->gld', heads_out, out_weight, precision=HIGH))
            normed_two = low(norm_rows(middle, gain_two, bias_two))
            upward = low_back(jnp.einsum('gld,df->glf', normed_two, up_weight, precision=HIGH) + up_bias)
            hidden = low(jax.nn.gelu(upward))
            mlp_out = jnp.einsum('glf,fd->gld', hidden, down_weight, precision=HIGH) + down_bias
            return jnp.where(is_valid[:, :, None], middle + mlp_out, 0.0)
        pieces = (token_rows.reshape(blocks, group, LMAX, D), time_rows.reshape(blocks, group, D), group_lengths)
        return lax.map(jax.checkpoint(one_group), pieces).reshape(TOKENS, D)
    result, pullback = jax.vjp(forward, *primals)
    grads = pullback(cotangent.astype(jnp.float32))
    return (result.astype(jnp.bfloat16), grads[0], grads[1], grads[2], grads[3], grads[4], grads[5], grads[6], grads[7], grads[8], grads[9], grads[10], grads[11], grads[12], grads[13], grads[14], grads[15], grads[16])
```

```python
import jax
import jax.numpy as jnp
from jax import lax
from jax.experimental import pallas as pl
from jax.experimental.pallas import tpu as pltpu
from jax.sharding import PartitionSpec as P


EPS = 1e-06
NEG = -1e30


def norm_rows(token_rows, norm_gain, norm_bias):
    centre = jnp.mean(token_rows, axis=-1, keepdims=True)
    centred = token_rows - centre
    spread = jnp.mean(centred * centred, axis=-1, keepdims=True)
    return centred * lax.rsqrt(spread + EPS) * norm_gain + norm_bias


def attend_scores(query_rows, key_rows, bias_rows, is_valid):
    score_scale = query_rows.shape[-1] ** (-0.5)
    scores = (
        jnp.einsum("bqhe,bkhe->bhqk", query_rows, key_rows, preferred_element_type=jnp.float32)
        * score_scale
        + bias_rows[None]
    )
    return jnp.where(is_valid[:, None, None, :], scores, NEG)


def forward_pass(weights, params, token_rows, time_rows, is_valid):
    (
        query_weight,
        key_weight,
        value_weight,
        query_time,
        value_time,
        out_weight,
        up_weight,
        down_weight,
    ) = weights
    gain_one, bias_one, gain_two, bias_two, up_bias, down_bias, bias_rows = params
    batch_size, seq_span, model_width = token_rows.shape
    heads_here = bias_rows.shape[0]
    normed_one = norm_rows(token_rows, gain_one, bias_one).astype(jnp.bfloat16)

    def project(weight, time_weight):
        direct = jnp.einsum("bld,de->ble", normed_one, weight, preferred_element_type=jnp.float32)
        from_time = jnp.dot(time_rows, time_weight, preferred_element_type=jnp.float32)
        return (
            (direct + from_time[:, None, :])
            .astype(jnp.bfloat16)
            .reshape(batch_size, seq_span, heads_here, -1)
        )

    query_rows = project(query_weight, query_time)
    key_direct = jnp.einsum(
        "bld,de->ble", normed_one, key_weight, preferred_element_type=jnp.float32
    )
    key_rows = key_direct.astype(jnp.bfloat16).reshape(batch_size, seq_span, heads_here, -1)
    value_rows = project(value_weight, value_time)
    scores = attend_scores(query_rows, key_rows, bias_rows, is_valid)
    highest = jnp.max(scores, axis=-1, keepdims=True)
    powers = jnp.exp(scores - highest)
    totals = jnp.sum(powers, axis=-1, keepdims=True)
    attn_probs = (powers / totals).astype(jnp.bfloat16)
    log_total = highest + jnp.log(totals)
    heads_out = jnp.einsum(
        "bhqk,bkhe->bqhe", attn_probs, value_rows, preferred_element_type=jnp.float32
    )
    heads_out = heads_out.astype(jnp.bfloat16).reshape(batch_size, seq_span, -1)
    partial_attn = jnp.einsum(
        "ble,ed->bld", heads_out, out_weight, preferred_element_type=jnp.float32
    )
    attn_part = lax.psum_scatter(
        partial_attn.astype(jnp.bfloat16), "mp", scatter_dimension=1, tiled=True
    ).astype(jnp.float32)
    middle = token_rows + lax.all_gather(
        attn_part.astype(jnp.bfloat16), "mp", axis=1, tiled=True
    ).astype(attn_part.dtype)
    normed_two = norm_rows(middle, gain_two, bias_two).astype(jnp.bfloat16)
    upward = (
        jnp.einsum("bld,df->blf", normed_two, up_weight, preferred_element_type=jnp.float32)
        + up_bias
    )
    hidden = jax.nn.gelu(upward).astype(jnp.bfloat16)
    partial_mlp = jnp.einsum("blf,fd->bld", hidden, down_weight, preferred_element_type=jnp.float32)
    mlp_part = lax.psum_scatter(
        partial_mlp.astype(jnp.bfloat16), "mp", scatter_dimension=1, tiled=True
    ).astype(jnp.float32)
    mlp_out = (
        lax.all_gather(mlp_part.astype(jnp.bfloat16), "mp", axis=1, tiled=True).astype(
            mlp_part.dtype
        )
        + down_bias
    )
    block_rows = jnp.where(is_valid[:, :, None], middle + mlp_out, 0.0).astype(jnp.bfloat16)
    stored = (
        normed_one,
        query_rows,
        key_rows,
        value_rows,
        log_total,
        heads_out,
        middle,
        normed_two,
        upward,
        hidden,
    )
    return (block_rows, stored)


def backward_pass(weights, params, token_rows, time_rows, is_valid, stored, grad_rows):
    (
        query_weight,
        key_weight,
        value_weight,
        query_time,
        value_time,
        out_weight,
        up_weight,
        down_weight,
    ) = weights
    gain_one, bias_one, gain_two, bias_two, up_bias, down_bias, bias_rows = params
    (
        normed_one,
        query_rows,
        key_rows,
        value_rows,
        log_total,
        heads_out,
        middle,
        normed_two,
        upward,
        hidden,
    ) = stored
    batch_size, seq_span, model_width = token_rows.shape
    heads_here = bias_rows.shape[0]
    grad_mix = jnp.where(is_valid[:, :, None], grad_rows, 0.0)
    mix_low = grad_mix.astype(jnp.bfloat16)
    grad_down = jnp.einsum("blf,bld->fd", hidden, mix_low, preferred_element_type=jnp.float32)
    grad_down_bias = jnp.sum(grad_mix, axis=(0, 1))
    grad_hidden = jnp.einsum(
        "bld,fd->blf", mix_low, down_weight, preferred_element_type=jnp.float32
    )
    gelu_back = jax.vjp(jax.nn.gelu, upward)[1]
    grad_upward = gelu_back(grad_hidden)[0].astype(jnp.bfloat16)
    grad_up = jnp.einsum("bld,blf->df", normed_two, grad_upward, preferred_element_type=jnp.float32)
    grad_up_bias = jnp.sum(grad_upward.astype(jnp.float32), axis=(0, 1))
    partial_two = jnp.einsum(
        "blf,df->bld", grad_upward, up_weight, preferred_element_type=jnp.float32
    )
    two_part = lax.psum_scatter(
        partial_two.astype(jnp.bfloat16), "mp", scatter_dimension=1, tiled=True
    ).astype(jnp.float32)
    grad_normed_two = lax.all_gather(
        two_part.astype(jnp.bfloat16), "mp", axis=1, tiled=True
    ).astype(two_part.dtype)
    norm_two_back = jax.vjp(norm_rows, middle, gain_two, bias_two)[1]
    grad_middle, grad_gain_two, grad_bias_two = norm_two_back(grad_normed_two)
    grad_middle = grad_middle + grad_mix
    middle_low = grad_middle.astype(jnp.bfloat16)
    grad_out = jnp.einsum("ble,bld->ed", heads_out, middle_low, preferred_element_type=jnp.float32)
    grad_heads = jnp.einsum(
        "bld,ed->ble", middle_low, out_weight, preferred_element_type=jnp.float32
    )
    grad_heads = grad_heads.astype(jnp.bfloat16).reshape(batch_size, seq_span, heads_here, -1)
    scores = attend_scores(query_rows, key_rows, bias_rows, is_valid)
    attn_probs = jnp.exp(scores - log_total)
    grad_probs = jnp.einsum(
        "bqhe,bkhe->bhqk", grad_heads, value_rows, preferred_element_type=jnp.float32
    )
    grad_value = jnp.einsum(
        "bhqk,bqhe->bkhe",
        attn_probs.astype(jnp.bfloat16),
        grad_heads,
        preferred_element_type=jnp.float32,
    )
    grad_value = grad_value.astype(jnp.bfloat16).reshape(batch_size, seq_span, -1)
    inner = jnp.sum(attn_probs * grad_probs, axis=-1, keepdims=True)
    grad_scores = (attn_probs * (grad_probs - inner)).astype(jnp.bfloat16)
    score_scale = query_rows.shape[-1] ** (-0.5)
    grad_query = (
        jnp.einsum("bhqk,bkhe->bqhe", grad_scores, key_rows, preferred_element_type=jnp.float32)
        * score_scale
    )
    grad_query = grad_query.astype(jnp.bfloat16).reshape(batch_size, seq_span, -1)
    grad_key = (
        jnp.einsum("bhqk,bqhe->bkhe", grad_scores, query_rows, preferred_element_type=jnp.float32)
        * score_scale
    )
    grad_key = grad_key.astype(jnp.bfloat16).reshape(batch_size, seq_span, -1)
    grad_bias_rows = jnp.sum(grad_scores.astype(jnp.float32), axis=0)

    def weight_grad(grad_proj):
        return jnp.einsum("bld,ble->de", normed_one, grad_proj, preferred_element_type=jnp.float32)

    def time_grad(grad_proj):
        return jnp.einsum("bd,ble->de", time_rows, grad_proj, preferred_element_type=jnp.float32)

    def back_rows(grad_proj, weight):
        return jnp.einsum("ble,de->bld", grad_proj, weight, preferred_element_type=jnp.float32)

    def back_time(grad_proj, time_weight):
        return jnp.einsum("ble,de->bd", grad_proj, time_weight, preferred_element_type=jnp.float32)

    part_one = (
        back_rows(grad_query, query_weight)
        + back_rows(grad_key, key_weight)
        + back_rows(grad_value, value_weight)
    )
    part_time = back_time(grad_query, query_time) + back_time(grad_value, value_time)
    one_share, time_share = (
        lax.psum_scatter(
            part_one.astype(jnp.bfloat16), "mp", scatter_dimension=1, tiled=True
        ).astype(jnp.float32),
        lax.psum_scatter(
            part_time.astype(jnp.bfloat16), "mp", scatter_dimension=1, tiled=True
        ).astype(jnp.float32),
    )
    grad_normed_one, grad_time = (
        lax.all_gather(one_share.astype(jnp.bfloat16), "mp", axis=1, tiled=True).astype(
            one_share.dtype
        ),
        lax.all_gather(time_share.astype(jnp.bfloat16), "mp", axis=1, tiled=True).astype(
            time_share.dtype
        ),
    )
    norm_one_back = jax.vjp(norm_rows, token_rows, gain_one, bias_one)[1]
    grad_token, grad_gain_one, grad_bias_one = norm_one_back(grad_normed_one)
    grad_input = grad_middle + grad_token
    matrix_grads = (
        weight_grad(grad_query),
        weight_grad(grad_key),
        weight_grad(grad_value),
        time_grad(grad_query),
        time_grad(grad_value),
        grad_out,
        grad_up,
        grad_down,
    )
    small_grads = (
        grad_gain_one,
        grad_bias_one,
        grad_gain_two,
        grad_bias_two,
        grad_up_bias,
        grad_down_bias,
        grad_bias_rows,
    )
    return (matrix_grads, small_grads, grad_input, grad_time)


LANES = 128


def bias_gather_body(table_ref, index_ref, out_ref):
    heads_here, chunks, _ = table_ref.shape
    row_count, width = index_ref.shape
    step_rows = 40

    @pl.loop(0, row_count // step_rows)
    def _(step):
        rows = pl.ds(pl.multiple_of(step * step_rows, 8), step_rows)
        for tile in range(width // LANES):
            lanes = slice(tile * LANES, (tile + 1) * LANES)
            entry = index_ref[rows, lanes]
            low = lax.bitwise_and(entry, LANES - 1)
            high = lax.shift_right_logical(entry, 7)
            for head in range(heads_here):
                found = jnp.zeros(entry.shape, jnp.float32)
                for chunk in range(chunks):
                    source = jnp.broadcast_to(table_ref[head, chunk : chunk + 1, :], entry.shape)
                    picked = jnp.take_along_axis(source, low, axis=1, mode="promise_in_bounds")
                    found = jnp.where(high == chunk, picked, found)
                out_ref[head, rows, lanes] = found


def bias_scatter_body(grad_ref, index_ref, out_ref):
    heads_here, row_count, width = grad_ref.shape
    high_row = lax.broadcasted_iota(jnp.int32, (8, width), 0)
    low_row = lax.broadcasted_iota(jnp.int32, (LANES, width), 0)

    def step(block, total):
        rows = pl.ds(pl.multiple_of(block * 8, 8), 8)
        entry = index_ref[rows, :]
        low = lax.bitwise_and(entry, LANES - 1)
        high = lax.shift_right_logical(entry, 7)
        grads = [grad_ref[head, rows, :] for head in range(heads_here)]
        for row in range(8):
            hit = high_row == jnp.broadcast_to(high[row : row + 1], (8, width))
            left = jnp.concatenate(
                [
                    jnp.where(hit, jnp.broadcast_to(grad[row : row + 1], (8, width)), 0.0)
                    for grad in grads
                ],
                axis=0,
            )
            right = jnp.where(
                low_row == jnp.broadcast_to(low[row : row + 1], (LANES, width)), 1.0, 0.0
            )
            total = total + lax.dot_general(
                left.astype(jnp.bfloat16),
                right.astype(jnp.bfloat16),
                (((1,), (1,)), ((), ())),
                preferred_element_type=jnp.float32,
            )
        return total

    start = jnp.zeros((heads_here * 8, LANES), jnp.float32)
    out_ref[...] = lax.fori_loop(0, row_count // 8, step, start)


def padded_index(rel_index):
    span = rel_index.shape[1]
    width = -(-span // LANES) * LANES
    return jnp.pad(rel_index, ((0, 0), (0, width - span)), constant_values=8 * LANES - 1)


def bias_gather(bias_table, index_wide):
    heads_here, entries = bias_table.shape
    table = jnp.pad(bias_table, ((0, 0), (0, 8 * LANES - entries))).reshape(heads_here, 8, LANES)
    return pl.pallas_call(
        bias_gather_body,
        out_shape=jax.ShapeDtypeStruct((heads_here,) + index_wide.shape, jnp.float32),
        name="bias_gather",
    )(table, index_wide)


def bias_scatter(grad_rows, index_wide, entries):
    heads_here = grad_rows.shape[0]
    sums = pl.pallas_call(
        bias_scatter_body,
        out_shape=jax.ShapeDtypeStruct((heads_here * 8, LANES), jnp.float32),
        name="bias_scatter",
    )(grad_rows, index_wide)
    return sums.reshape(heads_here, 8 * LANES)[:, :entries]


def on_device(
    tokens,
    time_token,
    lengths,
    rel_index,
    w_query,
    w_key,
    w_value,
    t_query,
    t_value,
    w_out,
    w_up,
    w_down,
    b_up,
    b_down,
    ln1_gain,
    ln1_bias,
    ln2_gain,
    ln2_bias,
    bias_table,
    cotangent,
):
    image_count = time_token.shape[0]
    seq_span = rel_index.shape[0]
    model_width = tokens.shape[1]
    index_wide = padded_index(rel_index)
    bias_wide = bias_gather(bias_table, index_wide)
    bias_rows = bias_wide[:, :, :seq_span]
    params = (ln1_gain, ln1_bias, ln2_gain, ln2_bias, b_up, b_down, bias_rows)
    token_rows = tokens.astype(jnp.float32).reshape(image_count, seq_span, model_width)
    grad_rows = cotangent.astype(jnp.float32).reshape(image_count, seq_span, model_width)
    is_valid = jnp.arange(seq_span)[None, :] < lengths[:, None]
    own = jnp.concatenate(
        [w_query, w_key, w_value, t_query, t_value, w_out.T, w_up, w_down.T], axis=1
    )
    widths = (
        w_query.shape[1],
        w_key.shape[1],
        w_value.shape[1],
        t_query.shape[1],
        t_value.shape[1],
        w_out.shape[0],
        w_up.shape[1],
        w_down.shape[0],
    )
    cuts = [sum(widths[: at + 1]) for at in range(len(widths) - 1)]
    whole = lax.all_gather(own, "dp", axis=0, tiled=True)
    pieces = jnp.split(whole, cuts, axis=1)
    weights = tuple(pieces[:5]) + (pieces[5].T, pieces[6], pieces[7].T)
    block_rows, stored = forward_pass(weights, params, token_rows, time_token, is_valid)
    matrix_grads, small_grads, grad_input, grad_time = backward_pass(
        weights, params, token_rows, time_token, is_valid, stored, grad_rows
    )
    turned = tuple(matrix_grads[:5]) + (matrix_grads[5].T, matrix_grads[6], matrix_grads[7].T)
    joined = jnp.concatenate([entry.astype(jnp.bfloat16) for entry in turned], axis=1)
    share = lax.psum_scatter(joined, "dp", scatter_dimension=0, tiled=True).astype(jnp.float32)
    shares = jnp.split(share, cuts, axis=1)
    shares[5] = shares[5].T
    shares[7] = shares[7].T
    bias_grads = jnp.pad(
        small_grads[6], ((0, 0), (0, 0), (0, index_wide.shape[1] - seq_span))
    )
    table_grad = bias_scatter(bias_grads, index_wide, bias_table.shape[1])
    summed = lax.psum(tuple(small_grads[:6]) + (table_grad,), "dp")
    return (
        block_rows.reshape(-1, model_width),
        grad_input.reshape(-1, model_width),
        grad_time,
        *shares,
        summed[4],
        summed[5],
        summed[0],
        summed[1],
        summed[2],
        summed[3],
        summed[6],
    )


def solution(mesh):
    placed = (
        P("dp", None),
        P("dp", None),
        P("dp"),
        P(),
        P("dp", "mp"),
        P("dp", "mp"),
        P("dp", "mp"),
        P("dp", "mp"),
        P("dp", "mp"),
        P("mp", "dp"),
        P("dp", "mp"),
        P("mp", "dp"),
        P("mp"),
        P(),
        P(),
        P(),
        P(),
        P(),
        P("mp", None),
        P("dp", None),
    )
    return jax.shard_map(
        on_device,
        mesh=mesh,
        in_specs=placed,
        out_specs=(
            P("dp", None),
            P("dp", None),
            P("dp", None),
            P("dp", "mp"),
            P("dp", "mp"),
            P("dp", "mp"),
            P("dp", "mp"),
            P("dp", "mp"),
            P("mp", "dp"),
            P("dp", "mp"),
            P("mp", "dp"),
            P("mp"),
            P(),
            P(),
            P(),
            P(),
            P(),
            P("mp", None),
        ),
        check_vma=False,
    )
```
